32 devices in a mesh: gx: 4 (over z), gy: 8 (over y, x, core).
Axes of the slice: x: 2, y: 2, z: 4, core: 2. Of those that a mesh axis runs over, the one named last changes fastest.
Arguments:
- seismic: float32 [512, 512, 256], P('gx', 'gy'), may hold values from -41 to 41, as said below
Outputs:
- shift_field: float32 [512, 512, 256], P('gx', 'gy')
- residual: float32 [512, 512, 256], P('gx', 'gy')
The draws below stay inside these ranges and needn't reach their ends.
Inputs may be any that keep to these rules, and one draw needn't show every extreme that they name: `seismic`: recorded amplitudes of the window.
All inputs are finite; a program needn't handle non-finite values.
Results may differ from the reference program's by a relative error of at most 0.0003.
Values sent between devices are 32-bit elements; how exact they have to be, the bound alone decides.
A program may use at most 320 MiB of HBM per device.

```python
import math
import jax
import jax.numpy as jnp
from jax import lax

NX = 512
NY = 512
NT = 256
ITERS = 2


def draw_seismic(key, part):
    noise_key, trace_key = jax.random.split(jax.random.fold_in(key, 11), 2)
    xs = jnp.arange(NX, dtype=jnp.float32)[:, None, None]
    ys = jnp.arange(NY, dtype=jnp.float32)[None, :, None]
    ts = jnp.arange(NT, dtype=jnp.float32)[None, None, :]
    amplitude = 0.5 * jnp.exp(math.log(9.0) * 0.5 * (xs / NX + ys / NY))
    trace_gain = jnp.exp(jax.random.uniform(trace_key, (NX, NY, 1), jnp.float32, 0.0, math.log(2.0)))
    noise = jax.random.truncated_normal(noise_key, -4.0, 4.0, (NX, NY, NT), jnp.float32)
    event = jnp.cos(2.0 * math.pi * (ts - 0.08 * xs - 0.12 * ys) / 17.0)
    return (amplitude * (trace_gain * noise + event)).astype(jnp.float32)


def setup_inputs(seed: int = 0) -> dict:
    splits = jax.random.split(jax.random.key(seed), 2)
    return {
        "seismic": draw_seismic(jax.random.fold_in(splits[1], 71), 0),
    }


damping = 0.001
floor_term = 0.5
highest = lax.Precision.HIGHEST

def cut(field, start, stop, axis):
    return lax.slice_in_dim(field, start, stop, axis=axis)

def smooth_axis(field, axis):
    length = field.shape[axis]
    return 0.25 * (cut(field, 0, length - 2, axis) + 2.0 * cut(field, 1, length - 1, axis) + cut(field, 2, length, axis))

def pad_time(field):
    return jnp.pad(field, ((0, 0), (0, 0), (1, 1)))

def smooth_all(field):
    return smooth_axis(pad_time(smooth_axis(smooth_axis(field, 0), 1)), 2)

def tensor_fields(padded, inside_x, inside_y):
    mask = inside_x[:, None, None] * inside_y[None, :, None]
    grad_x = 0.5 * (padded[2:, 1:-1] - padded[:-2, 1:-1]) * mask
    grad_y = 0.5 * (padded[1:-1, 2:] - padded[1:-1, :-2]) * mask
    timed = pad_time(padded[1:-1, 1:-1])
    grad_t = 0.5 * (timed[:, :, 2:] - timed[:, :, :-2]) * mask
    cross_x = smooth_all(grad_x * grad_t)
    cross_y = smooth_all(grad_y * grad_t)
    along_t = smooth_all(grad_t * grad_t) + floor_term
    spread = smooth_all(grad_x * grad_x + grad_y * grad_y)
    return (-cross_x / along_t, -cross_y / along_t, along_t / (along_t + spread))

def lower_of(field, axis):
    widths = [(0, 0), (0, 0), (0, 0)]
    widths[axis] = (1, 0)
    return cut(jnp.pad(field, widths), 0, field.shape[axis], axis)

def cosine_table(order):
    freq = jnp.arange(order, dtype=jnp.float32)[:, None]
    place = jnp.arange(order, dtype=jnp.float32)[None, :]
    scale = jnp.where(freq == 0.0, jnp.sqrt(1.0 / order), jnp.sqrt(2.0 / order)).astype(jnp.float32)
    return (scale * jnp.cos(jnp.pi * (place + 0.5) * freq / order)).astype(jnp.float32)

def eigen_values(order):
    freq = jnp.arange(order, dtype=jnp.float32)
    return (2.0 - 2.0 * jnp.cos(jnp.pi * freq / order)).astype(jnp.float32)

def operate(field, weight_x, weight_y, prior_x, prior_y):
    padded = jnp.pad(field, ((1, 1), (1, 1), (0, 0)))
    upper_x = padded[2:, 1:-1]
    lower_x = padded[:-2, 1:-1]
    upper_y = padded[1:-1, 2:]
    lower_y = padded[1:-1, :-2]
    return damping * field + weight_x * (field - upper_x) + prior_x * (field - lower_x) + weight_y * (field - upper_y) + prior_y * (field - lower_y)

def reference(seismic):
    table_x = cosine_table(NX)
    table_y = cosine_table(NY)
    denom = damping + eigen_values(NX)[:, None, None] + eigen_values(NY)[None, :, None]

    def precondition(field):
        hat = jnp.einsum('ki,ijt->kjt', table_x, field, precision=highest)
        hat = jnp.einsum('lj,kjt->klt', table_y, hat, precision=highest)
        hat = hat / denom
        hat = jnp.einsum('lj,klt->kjt', table_y, hat, precision=highest)
        return jnp.einsum('ki,kjt->ijt', table_x, hat, precision=highest)
    block = min(64, NX)
    padded = jnp.pad(seismic, ((2, 2), (2, 2), (0, 0)))
    grid_y = jnp.arange(-1, NY + 1, dtype=jnp.int32)
    inside_y = ((grid_y >= 0) & (grid_y < NY)).astype(jnp.float32)
    pieces = []
    for start in range(0, NX, block):
        grid_x = jnp.arange(start - 1, start + block + 1, dtype=jnp.int32)
        inside_x = ((grid_x >= 0) & (grid_x < NX)).astype(jnp.float32)
        pieces.append(tensor_fields(padded[start:start + block + 4], inside_x, inside_y))
    dip_x = jnp.concatenate([piece[0] for piece in pieces], 0)
    dip_y = jnp.concatenate([piece[1] for piece in pieces], 0)
    weight = jnp.concatenate([piece[2] for piece in pieces], 0)
    keep_x = (jnp.arange(NX, dtype=jnp.int32) < NX - 1).astype(jnp.float32)
    keep_y = (jnp.arange(NY, dtype=jnp.int32) < NY - 1).astype(jnp.float32)
    weight_x = weight * keep_x[:, None, None]
    weight_y = weight * keep_y[None, :, None]
    flux_x = weight_x * dip_x
    flux_y = weight_y * dip_y
    rhs = lower_of(flux_x, 0) - flux_x + (lower_of(flux_y, 1) - flux_y)
    prior_x = lower_of(weight_x, 0)
    prior_y = lower_of(weight_y, 1)
    shift_field = jnp.zeros_like(rhs)
    residual = rhs
    precond = precondition(residual)
    direction = precond
    norm_now = jnp.sum(residual * precond)
    for step in range(ITERS):
        image = operate(direction, weight_x, weight_y, prior_x, prior_y)
        alpha = norm_now / jnp.sum(direction * image)
        shift_field = shift_field + alpha * direction
        residual = residual - alpha * image
        if step + 1 < ITERS:
            precond = precondition(residual)
            norm_next = jnp.sum(residual * precond)
            direction = precond + norm_next / norm_now * direction
            norm_now = norm_next
    return (shift_field, residual)
```

```python
import jax
import jax.numpy as jnp
import numpy as np
from jax import lax
from jax.sharding import PartitionSpec as P

NX = 512
NY = 512
ITERS = 2


damping = 0.001
floor_term = 0.5
highest = lax.Precision.HIGHEST


def extended(block, sides, width):
    for axis, dim in sides:
        count = lax.axis_size(axis)
        forward = [(i, i + 1) for i in range(count - 1)]
        backward = [(target, source) for source, target in forward]
        low = lax.ppermute(
            lax.slice_in_dim(block, block.shape[dim] - width, None, axis=dim), axis, forward
        )
        high = lax.ppermute(lax.slice_in_dim(block, 0, width, axis=dim), axis, backward)
        block = jnp.concatenate([low, block, high], axis=dim)
    return block


def cut(field, start, stop, axis):
    return lax.slice_in_dim(field, start, stop, axis=axis)


def smooth_axis(field, axis):
    length = field.shape[axis]
    return 0.25 * (
        cut(field, 0, length - 2, axis)
        + 2.0 * cut(field, 1, length - 1, axis)
        + cut(field, 2, length, axis)
    )


def pad_time(field):
    return jnp.pad(field, ((0, 0), (0, 0), (1, 1)))


def smooth_all(field):
    return smooth_axis(pad_time(smooth_axis(smooth_axis(field, 0), 1)), 2)


def tensor_fields(padded, inside_x, inside_y):
    mask = inside_x[:, None, None] * inside_y[None, :, None]
    grad_x = 0.5 * (padded[2:, 1:-1] - padded[:-2, 1:-1]) * mask
    grad_y = 0.5 * (padded[1:-1, 2:] - padded[1:-1, :-2]) * mask
    timed = pad_time(padded[1:-1, 1:-1])
    grad_t = 0.5 * (timed[:, :, 2:] - timed[:, :, :-2]) * mask
    cross_x = smooth_all(grad_x * grad_t)
    cross_y = smooth_all(grad_y * grad_t)
    along_t = smooth_all(grad_t * grad_t) + floor_term
    spread = smooth_all(grad_x * grad_x + grad_y * grad_y)
    return (-cross_x / along_t, -cross_y / along_t, along_t / (along_t + spread))


def cosine_table(order):
    freq = np.arange(order, dtype=np.float64)[:, None]
    place = np.arange(order, dtype=np.float64)[None, :]
    scale = np.where(freq == 0.0, np.sqrt(1.0 / order), np.sqrt(2.0 / order))
    return scale * np.cos(np.pi * (place + 0.5) * freq / order)


def eigen_values(order):
    return 2.0 - 2.0 * np.cos(np.pi * np.arange(order, dtype=np.float64) / order)


def axis_tables(order, parts):
    rows = order // parts
    whole = cosine_table(order)
    local = cosine_table(rows)
    lift = np.concatenate(
        [local @ whole[:, part * rows : (part + 1) * rows].T for part in range(parts)], axis=0
    )
    ends = np.arange(1, parts) * rows - 1
    jump = (whole[:, ends] - whole[:, ends + 1]).T
    return local, eigen_values(rows), lift, jump


def solver_tables(order_x, order_y, parts_x, parts_y):
    local_x, near_x, lift_x, jump_x = axis_tables(order_x, parts_x)
    local_y, near_y, lift_y, jump_y = axis_tables(order_y, parts_y)
    inverse = 1.0 / (damping + eigen_values(order_x)[:, None] + eigen_values(order_y)[None, :])
    tables = {
        "local_x": local_x,
        "local_y": local_y,
        "near": 1.0 / (damping + near_x[:, None] + near_y[None, :]),
        "lift_x": lift_x,
        "lift_y": lift_y,
        "jump_x": jump_x,
        "jump_y": jump_y,
        "inverse": inverse,
        "self_x": np.einsum("ak,bk,kl->abl", jump_x, jump_x, inverse, optimize=True),
        "self_y": np.einsum("al,bl,kl->abk", jump_y, jump_y, inverse, optimize=True),
    }
    return {name: jnp.asarray(value.astype(np.float32)) for name, value in tables.items()}


def product(first, second):
    return lax.dot_general(
        first,
        second,
        (((first.ndim - 1,), (0,)), ((), ())),
        precision=highest,
        preferred_element_type=jnp.float32,
    )


def solve_borders(jumps_x, jumps_y, tables):
    hat_x = product(jumps_x, tables["lift_y"])
    hat_y = product(jumps_y, tables["lift_x"])
    jump_x, jump_y = tables["jump_x"], tables["jump_y"]
    cross_x = product(jump_x[:, None, None, :] * hat_y[None], tables["inverse"])
    cross_y = product(jump_y[None, :, None, :] * hat_x[:, None], tables["inverse"].T)
    flux_x = (
        hat_x
        - jnp.sum(tables["self_x"][:, :, None, :] * hat_x[None], axis=1)
        - jnp.sum(jump_y[None, :, None, :] * cross_x, axis=1)
    )
    flux_y = (
        hat_y
        - jnp.sum(tables["self_y"][:, :, None, :] * hat_y[None], axis=1)
        - jnp.sum(jump_x[:, None, None, :] * cross_y, axis=0)
    )
    return product(flux_x, tables["lift_y"].T), product(flux_y, tables["lift_x"].T)


def exchange(rows):
    return lax.all_to_all(rows, ("gx", "gy"), split_axis=0, concat_axis=0, tiled=True)


def forward(field, tables):
    hat = jnp.einsum("ki,ijt->kjt", tables["local_x"], field, precision=highest)
    return jnp.einsum("lj,kjt->klt", tables["local_y"], hat, precision=highest)


def backward(hat, tables):
    field = jnp.einsum("lj,klt->kjt", tables["local_y"], hat, precision=highest)
    return jnp.einsum("ki,kjt->ijt", tables["local_x"], field, precision=highest)


def precondition(field, tables, parts_x, parts_y):
    rows_x, rows_y, depth = field.shape
    per = depth // (parts_x * parts_y)
    near = tables["near"][:, :, None]
    first_x, last_x = tables["local_x"][:, 0], tables["local_x"][:, -1]
    first_y, last_y = tables["local_y"][:, 0], tables["local_y"][:, -1]
    hat = forward(field, tables)
    free = hat * near
    edges = jnp.concatenate(
        [
            jnp.sum(free * first_x[:, None, None], axis=0),
            jnp.sum(free * last_x[:, None, None], axis=0),
            jnp.sum(free * first_y[None, :, None], axis=1),
            jnp.sum(free * last_y[None, :, None], axis=1),
        ],
        axis=0,
    )
    got = exchange(edges.T).reshape(parts_x, parts_y, per, 2 * rows_x + 2 * rows_y)
    low_x, high_x = got[..., :rows_y], got[..., rows_y : 2 * rows_y]
    low_y, high_y = got[..., 2 * rows_y : 2 * rows_y + rows_x], got[..., 2 * rows_y + rows_x :]
    jumps_x = (high_x[:-1] - low_x[1:]).transpose(0, 2, 1, 3)
    jumps_y = (high_y[:, :-1] - low_y[:, 1:]).transpose(1, 2, 0, 3)
    flux_x, flux_y = solve_borders(
        jumps_x.reshape(parts_x - 1, per, -1), jumps_y.reshape(parts_y - 1, per, -1), tables
    )
    flux_x = flux_x.reshape(parts_x - 1, per, parts_y, rows_y).transpose(0, 2, 1, 3)
    flux_y = flux_y.reshape(parts_y - 1, per, parts_x, rows_x).transpose(2, 0, 1, 3)
    sent = jnp.concatenate(
        [
            jnp.pad(-flux_x, ((1, 0), (0, 0), (0, 0), (0, 0))),
            jnp.pad(flux_x, ((0, 1), (0, 0), (0, 0), (0, 0))),
            jnp.pad(-flux_y, ((0, 0), (1, 0), (0, 0), (0, 0))),
            jnp.pad(flux_y, ((0, 0), (0, 1), (0, 0), (0, 0))),
        ],
        axis=-1,
    )
    back = exchange(sent.reshape(depth, -1)).T
    solved = near * (
        hat
        - first_x[:, None, None] * back[None, :rows_y]
        - last_x[:, None, None] * back[None, rows_y : 2 * rows_y]
        - first_y[None, :, None] * back[2 * rows_y : 2 * rows_y + rows_x, None]
        - last_y[None, :, None] * back[2 * rows_y + rows_x :, None]
    )
    norm = lax.psum(jnp.sum(hat * solved), ("gx", "gy"))
    return backward(solved, tables), norm


def combine_terms(field, upper_x, lower_x, upper_y, lower_y, weight_x, weight_y, prior_x, prior_y):
    return (
        damping * field
        + weight_x * (field - upper_x)
        + prior_x * (field - lower_x)
        + weight_y * (field - upper_y)
        + prior_y * (field - lower_y)
    )


def operate(field, weight_x, weight_y, prior_x, prior_y):
    padded = extended(field, (("gx", 0), ("gy", 1)), 1)
    return combine_terms(
        field,
        padded[2:, 1:-1],
        padded[:-2, 1:-1],
        padded[1:-1, 2:],
        padded[1:-1, :-2],
        weight_x,
        weight_y,
        prior_x,
        prior_y,
    )


def solve(rhs, apply_op, precond_op):
    residual = rhs
    direction, norm_now = precond_op(residual)
    shift_field = None
    for step in range(ITERS):
        image = apply_op(direction)
        alpha = norm_now / lax.psum(jnp.sum(direction * image), ("gx", "gy"))
        moved = alpha * direction
        shift_field = moved if shift_field is None else shift_field + moved
        residual = residual - alpha * image
        if step + 1 < ITERS:
            precond, norm_next = precond_op(residual)
            direction = precond + norm_next / norm_now * direction
            norm_now = norm_next
    return (shift_field, residual)


def per_device(seismic):
    rows_x, rows_y, depth = seismic.shape
    parts_x = lax.axis_size("gx")
    parts_y = lax.axis_size("gy")
    base_x = lax.axis_index("gx") * rows_x
    base_y = lax.axis_index("gy") * rows_y
    tables = solver_tables(rows_x * parts_x, rows_y * parts_y, parts_x, parts_y)
    padded = extended(seismic, (("gx", 0), ("gy", 1)), 3)
    grid_x = base_x + jnp.arange(-2, rows_x + 2, dtype=jnp.int32)
    grid_y = base_y + jnp.arange(-2, rows_y + 2, dtype=jnp.int32)
    inside_x = ((grid_x >= 0) & (grid_x < NX)).astype(jnp.float32)
    inside_y = ((grid_y >= 0) & (grid_y < NY)).astype(jnp.float32)
    dip_x, dip_y, weight = tensor_fields(padded, inside_x, inside_y)
    edge_x = grid_x[1:-1]
    edge_y = grid_y[1:-1]
    keep_x = ((edge_x >= 0) & (edge_x < NX - 1)).astype(jnp.float32)
    keep_y = ((edge_y >= 0) & (edge_y < NY - 1)).astype(jnp.float32)
    weight_x = weight * keep_x[:, None, None]
    weight_y = weight * keep_y[None, :, None]
    flux_x = weight_x * dip_x
    flux_y = weight_y * dip_y
    rhs = flux_x[:-2, 1:-1] - flux_x[1:-1, 1:-1] + (flux_y[1:-1, :-2] - flux_y[1:-1, 1:-1])
    own_x = weight_x[1:-1, 1:-1]
    prior_x = weight_x[:-2, 1:-1]
    own_y = weight_y[1:-1, 1:-1]
    prior_y = weight_y[1:-1, :-2]

    def precond_op(field):
        return precondition(field, tables, parts_x, parts_y)

    def apply_tiles(field):
        return operate(field, own_x, own_y, prior_x, prior_y)

    return solve(rhs, apply_tiles, precond_op)


def solution(mesh):
    placed = (P("gx", "gy", None),)
    return jax.shard_map(
        per_device,
        mesh=mesh,
        in_specs=placed,
        out_specs=(P("gx", "gy", None), P("gx", "gy", None)),
        check_vma=False,
    )
```

```python
import jax
import jax.numpy as jnp
import numpy as np
from jax import lax
from jax.sharding import PartitionSpec as P

NX = 512
NY = 512
ITERS = 2


damping = 0.001
floor_term = 0.5
highest = lax.Precision.HIGHEST


def extended(block, sides, width):
    for axis, dim in sides:
        count = lax.axis_size(axis)
        forward = [(i, i + 1) for i in range(count - 1)]
        backward = [(target, source) for source, target in forward]
        low = lax.ppermute(
            lax.slice_in_dim(block, block.shape[dim] - width, None, axis=dim), axis, forward
        )
        high = lax.ppermute(lax.slice_in_dim(block, 0, width, axis=dim), axis, backward)
        block = jnp.concatenate([low, block, high], axis=dim)
    return block


def cut(field, start, stop, axis):
    return lax.slice_in_dim(field, start, stop, axis=axis)


def smooth_axis(field, axis):
    length = field.shape[axis]
    return 0.25 * (
        cut(field, 0, length - 2, axis)
        + 2.0 * cut(field, 1, length - 1, axis)
        + cut(field, 2, length, axis)
    )


def pad_time(field):
    return jnp.pad(field, ((0, 0), (0, 0), (1, 1)))


def smooth_all(field):
    return smooth_axis(pad_time(smooth_axis(smooth_axis(field, 0), 1)), 2)


def tensor_fields(padded, inside_x, inside_y):
    mask = inside_x[:, None, None] * inside_y[None, :, None]
    grad_x = 0.5 * (padded[2:, 1:-1] - padded[:-2, 1:-1]) * mask
    grad_y = 0.5 * (padded[1:-1, 2:] - padded[1:-1, :-2]) * mask
    timed = pad_time(padded[1:-1, 1:-1])
    grad_t = 0.5 * (timed[:, :, 2:] - timed[:, :, :-2]) * mask
    cross_x = smooth_all(grad_x * grad_t)
    cross_y = smooth_all(grad_y * grad_t)
    along_t = smooth_all(grad_t * grad_t) + floor_term
    spread = smooth_all(grad_x * grad_x + grad_y * grad_y)
    return (-cross_x / along_t, -cross_y / along_t, along_t / (along_t + spread))


def cosine_table(order):
    freq = np.arange(order, dtype=np.float64)[:, None]
    place = np.arange(order, dtype=np.float64)[None, :]
    scale = np.where(freq == 0.0, np.sqrt(1.0 / order), np.sqrt(2.0 / order))
    return scale * np.cos(np.pi * (place + 0.5) * freq / order)


def eigen_values(order):
    return 2.0 - 2.0 * np.cos(np.pi * np.arange(order, dtype=np.float64) / order)


def axis_tables(order, parts):
    rows = order // parts
    whole = cosine_table(order)
    local = cosine_table(rows)
    lift = np.concatenate(
        [local @ whole[:, part * rows : (part + 1) * rows].T for part in range(parts)], axis=0
    )
    ends = np.arange(1, parts) * rows - 1
    jump = (whole[:, ends] - whole[:, ends + 1]).T
    return local, eigen_values(rows), lift, jump


def solver_tables(order_x, order_y, parts_x, parts_y):
    local_x, near_x, lift_x, jump_x = axis_tables(order_x, parts_x)
    local_y, near_y, lift_y, jump_y = axis_tables(order_y, parts_y)
    inverse = 1.0 / (damping + eigen_values(order_x)[:, None] + eigen_values(order_y)[None, :])
    tables = {
        "local_x": local_x,
        "local_y": local_y,
        "near": 1.0 / (damping + near_x[:, None] + near_y[None, :]),
        "lift_x": lift_x,
        "lift_y": lift_y,
        "jump_x": jump_x,
        "jump_y": jump_y,
        "inverse": inverse,
        "self_x": np.einsum("ak,bk,kl->abl", jump_x, jump_x, inverse, optimize=True),
        "self_y": np.einsum("al,bl,kl->abk", jump_y, jump_y, inverse, optimize=True),
    }
    return {name: jnp.asarray(value.astype(np.float32)) for name, value in tables.items()}


def product(first, second):
    return lax.dot_general(
        first,
        second,
        (((first.ndim - 1,), (0,)), ((), ())),
        precision=highest,
        preferred_element_type=jnp.float32,
    )


def solve_borders(jumps_x, jumps_y, tables):
    hat_x = product(jumps_x, tables["lift_y"])
    hat_y = product(jumps_y, tables["lift_x"])
    jump_x, jump_y = tables["jump_x"], tables["jump_y"]
    cross_x = product(jump_x[:, None, None, :] * hat_y[None], tables["inverse"])
    cross_y = product(jump_y[None, :, None, :] * hat_x[:, None], tables["inverse"].T)
    flux_x = (
        hat_x
        - jnp.sum(tables["self_x"][:, :, None, :] * hat_x[None], axis=1)
        - jnp.sum(jump_y[None, :, None, :] * cross_x, axis=1)
    )
    flux_y = (
        hat_y
        - jnp.sum(tables["self_y"][:, :, None, :] * hat_y[None], axis=1)
        - jnp.sum(jump_x[:, None, None, :] * cross_y, axis=0)
    )
    return product(flux_x, tables["lift_y"].T), product(flux_y, tables["lift_x"].T)


def exchange(rows):
    return lax.all_to_all(rows, ("gx", "gy"), split_axis=0, concat_axis=0, tiled=True)


def forward(field, tables):
    hat = jnp.einsum("ki,ijt->kjt", tables["local_x"], field, precision=highest)
    return jnp.einsum("lj,kjt->klt", tables["local_y"], hat, precision=highest)


def backward(hat, tables):
    field = jnp.einsum("lj,klt->kjt", tables["local_y"], hat, precision=highest)
    return jnp.einsum("ki,kjt->ijt", tables["local_x"], field, precision=highest)


def precondition(field, tables, parts_x, parts_y):
    rows_x, rows_y, depth = field.shape
    per = depth // (parts_x * parts_y)
    near = tables["near"][:, :, None]
    first_x, last_x = tables["local_x"][:, 0], tables["local_x"][:, -1]
    first_y, last_y = tables["local_y"][:, 0], tables["local_y"][:, -1]
    hat = forward(field, tables)
    free = hat * near
    edges = jnp.concatenate(
        [
            jnp.sum(free * first_x[:, None, None], axis=0),
            jnp.sum(free * last_x[:, None, None], axis=0),
            jnp.sum(free * first_y[None, :, None], axis=1),
            jnp.sum(free * last_y[None, :, None], axis=1),
        ],
        axis=0,
    )
    got = exchange(edges.T).reshape(parts_x, parts_y, per, 2 * rows_x + 2 * rows_y)
    low_x, high_x = got[..., :rows_y], got[..., rows_y : 2 * rows_y]
    low_y, high_y = got[..., 2 * rows_y : 2 * rows_y + rows_x], got[..., 2 * rows_y + rows_x :]
    jumps_x = (high_x[:-1] - low_x[1:]).transpose(0, 2, 1, 3)
    jumps_y = (high_y[:, :-1] - low_y[:, 1:]).transpose(1, 2, 0, 3)
    flux_x, flux_y = solve_borders(
        jumps_x.reshape(parts_x - 1, per, -1), jumps_y.reshape(parts_y - 1, per, -1), tables
    )
    flux_x = flux_x.reshape(parts_x - 1, per, parts_y, rows_y).transpose(0, 2, 1, 3)
    flux_y = flux_y.reshape(parts_y - 1, per, parts_x, rows_x).transpose(2, 0, 1, 3)
    sent = jnp.concatenate(
        [
            jnp.pad(-flux_x, ((1, 0), (0, 0), (0, 0), (0, 0))),
            jnp.pad(flux_x, ((0, 1), (0, 0), (0, 0), (0, 0))),
            jnp.pad(-flux_y, ((0, 0), (1, 0), (0, 0), (0, 0))),
            jnp.pad(flux_y, ((0, 0), (0, 1), (0, 0), (0, 0))),
        ],
        axis=-1,
    )
    back = exchange(sent.reshape(depth, -1)).T
    solved = near * (
        hat
        - first_x[:, None, None] * back[None, :rows_y]
        - last_x[:, None, None] * back[None, rows_y : 2 * rows_y]
        - first_y[None, :, None] * back[2 * rows_y : 2 * rows_y + rows_x, None]
        - last_y[None, :, None] * back[2 * rows_y + rows_x :, None]
    )
    return backward(solved, tables), jnp.sum(hat * solved)


def combine_terms(field, upper_x, lower_x, upper_y, lower_y, weight_x, weight_y, prior_x, prior_y):
    return (
        damping * field
        + weight_x * (field - upper_x)
        + prior_x * (field - lower_x)
        + weight_y * (field - upper_y)
        + prior_y * (field - lower_y)
    )


def operate(field, weight_x, weight_y, prior_x, prior_y):
    padded = extended(field, (("gx", 0), ("gy", 1)), 1)
    return combine_terms(
        field,
        padded[2:, 1:-1],
        padded[:-2, 1:-1],
        padded[1:-1, 2:],
        padded[1:-1, :-2],
        weight_x,
        weight_y,
        prior_x,
        prior_y,
    )


def totals(*partials):
    count = lax.axis_size("gx") * lax.axis_size("gy")
    rows = jnp.broadcast_to(jnp.stack(partials)[None, :, None], (count, len(partials), 128))
    return jnp.sum(exchange(rows), axis=0)[:, 0]


def solve(rhs, apply_op, precond_op):
    residual = rhs
    direction, part = precond_op(residual)
    norm_now = None
    shift_field = None
    for step in range(ITERS):
        image = apply_op(direction)
        curve = jnp.sum(direction * image)
        if norm_now is None:
            norm_now, curve = totals(part, curve)
        else:
            (curve,) = totals(curve)
        alpha = norm_now / curve
        moved = alpha * direction
        shift_field = moved if shift_field is None else shift_field + moved
        residual = residual - alpha * image
        if step + 1 < ITERS:
            precond, part = precond_op(residual)
            (norm_next,) = totals(part)
            direction = precond + norm_next / norm_now * direction
            norm_now = norm_next
    return (shift_field, residual)


def per_device(seismic):
    rows_x, rows_y, depth = seismic.shape
    parts_x = lax.axis_size("gx")
    parts_y = lax.axis_size("gy")
    base_x = lax.axis_index("gx") * rows_x
    base_y = lax.axis_index("gy") * rows_y
    tables = solver_tables(rows_x * parts_x, rows_y * parts_y, parts_x, parts_y)
    padded = extended(seismic, (("gx", 0), ("gy", 1)), 3)
    grid_x = base_x + jnp.arange(-2, rows_x + 2, dtype=jnp.int32)
    grid_y = base_y + jnp.arange(-2, rows_y + 2, dtype=jnp.int32)
    inside_x = ((grid_x >= 0) & (grid_x < NX)).astype(jnp.float32)
    inside_y = ((grid_y >= 0) & (grid_y < NY)).astype(jnp.float32)
    dip_x, dip_y, weight = tensor_fields(padded, inside_x, inside_y)
    edge_x = grid_x[1:-1]
    edge_y = grid_y[1:-1]
    keep_x = ((edge_x >= 0) & (edge_x < NX - 1)).astype(jnp.float32)
    keep_y = ((edge_y >= 0) & (edge_y < NY - 1)).astype(jnp.float32)
    weight_x = weight * keep_x[:, None, None]
    weight_y = weight * keep_y[None, :, None]
    flux_x = weight_x * dip_x
    flux_y = weight_y * dip_y
    rhs = flux_x[:-2, 1:-1] - flux_x[1:-1, 1:-1] + (flux_y[1:-1, :-2] - flux_y[1:-1, 1:-1])
    own_x = weight_x[1:-1, 1:-1]
    prior_x = weight_x[:-2, 1:-1]
    own_y = weight_y[1:-1, 1:-1]
    prior_y = weight_y[1:-1, :-2]

    def precond_op(field):
        return precondition(field, tables, parts_x, parts_y)

    def apply_tiles(field):
        return operate(field, own_x, own_y, prior_x, prior_y)

    return solve(rhs, apply_tiles, precond_op)


def solution(mesh):
    placed = (P("gx", "gy", None),)
    return jax.shard_map(
        per_device,
        mesh=mesh,
        in_specs=placed,
        out_specs=(P("gx", "gy", None), P("gx", "gy", None)),
        check_vma=False,
    )
```
